32 devices in a mesh: dp: 32 (over z, y, x, core).
Axes of the slice: x: 2, y: 2, z: 4, core: 2. Of those that a mesh axis runs over, the one named last changes fastest.
Arguments:
- activations: bfloat16 [65536, 512], P('dp'), may hold values from -6 to 6
- cotangent: float32 [65536, 512], P('dp'), may hold values from -6 to 6
- video_length: int32 [32, 2], replicated, may hold values from 204 to 1024, as said below
- mix_weight: float32 [4, 512, 512], P(None, 'dp'), may hold values from -1.06066017 to 1.06066017
- mix_first: float32 [4, 512, 512], P(None, 'dp'), may hold values from -0.00018310547 to 0.00018310547
- mix_second: float32 [4, 512, 512], P(None, 'dp'), may hold values from 1.373291e-11 to 5.493164e-11
- mix_average: float32 [4, 512, 512], P(None, 'dp'), may hold values from -0.25 to 0.25
- up_weight: float32 [512, 2048], P('dp'), may hold values from -0.25 to 0.25
- up_first: float32 [512, 2048], P('dp'), may hold values from -0.00018310547 to 0.00018310547
- up_second: float32 [512, 2048], P('dp'), may hold values from 1.373291e-11 to 5.493164e-11
- up_average: float32 [512, 2048], P('dp'), may hold values from -0.25 to 0.25
- down_weight: float32 [2048, 512], P('dp'), may hold values from -0.125 to 0.125
- down_first: float32 [2048, 512], P('dp'), may hold values from -0.00018310547 to 0.00018310547
- down_second: float32 [2048, 512], P('dp'), may hold values from 1.373291e-11 to 5.493164e-11
- down_average: float32 [2048, 512], P('dp'), may hold values from -0.125 to 0.125
- vector_weight: float32 [28, 512], P(None, 'dp'), may hold values from -3 to 3
- vector_first: float32 [28, 512], P(None, 'dp'), may hold values from -0.0007324219 to 0.0007324219
- vector_second: float32 [28, 512], P(None, 'dp'), may hold values from 2.1972656e-10 to 8.789062e-10
- vector_average: float32 [28, 512], P(None, 'dp'), may hold values from -4 to 4
Outputs:
- block_output: bfloat16 [65536, 512], P('dp')
- input_grad: float32 [65536, 512], P('dp')
- grad_norm: float32 [], replicated
- new_mix_weight: float32 [4, 512, 512], P(None, 'dp')
- new_mix_first: float32 [4, 512, 512], P(None, 'dp')
- new_mix_second: float32 [4, 512, 512], P(None, 'dp')
- new_mix_average: float32 [4, 512, 512], P(None, 'dp')
- new_up_weight: float32 [512, 2048], P('dp')
- new_up_first: float32 [512, 2048], P('dp')
- new_up_second: float32 [512, 2048], P('dp')
- new_up_average: float32 [512, 2048], P('dp')
- new_down_weight: float32 [2048, 512], P('dp')
- new_down_first: float32 [2048, 512], P('dp')
- new_down_second: float32 [2048, 512], P('dp')
- new_down_average: float32 [2048, 512], P('dp')
- new_vector_weight: float32 [28, 512], P(None, 'dp')
- new_vector_first: float32 [28, 512], P(None, 'dp')
- new_vector_second: float32 [28, 512], P(None, 'dp')
- new_vector_average: float32 [28, 512], P(None, 'dp')
- clipped_bias_grad: float32 [512], P('dp')
The draws below stay inside these ranges and needn't reach their ends.
Inputs may be any that keep to these rules, and one draw needn't show every extreme that they name: `video_length`: each of the 2 videos of a group has 204 to 1024 frames; in every draw some group holds 2 videos of 1024 frames.
All inputs are finite; a program needn't handle non-finite values.
Results may differ from the reference program's by a relative error of at most 0.007.
The reference program's roundings to bfloat16 on the way count: a program that leaves them out, or rounds other values in their place, can miss the bound.
Values may be sent and summed in bfloat16 or wider, within the bound.
A program may use at most 256 MiB of HBM per device.

```python
import math
import jax
import jax.numpy as jnp
from jax import lax

D = 512
FF = 2048
HEADS = 4
WINDOW = 19
SLOTS = 2
STEP = 10
FRAMES_DEV = 2048
HEAD = 128
MAXLEN = 1024
MINLEN = 204
GROUPS = 32
TOKENS = 65536
NVEC = 28
NPARAM = 3160064
N_DP = 32


def draw_video_length(key, part):
    key = jax.random.fold_in(key, 3)
    pick_key, full_key = jax.random.split(key)
    ranks = jnp.arange(GROUPS, dtype=jnp.int32)[:, None]
    lowest = MINLEN + (MAXLEN - MINLEN) * ranks // (2 * GROUPS)
    highest = MINLEN + (MAXLEN - MINLEN) * (ranks + 1) // GROUPS
    raw_bits = jax.random.randint(pick_key, (GROUPS, SLOTS), 0, 1 << 20)
    lengths = lowest + raw_bits % (highest - lowest + 1)
    fullest = jax.random.randint(full_key, (), GROUPS // 2, GROUPS)
    return jnp.where(ranks == fullest, MAXLEN, lengths).astype(jnp.int32)


def draw_mix_weight(key, part):
    key = jax.random.fold_in(key, 5)
    fans = jnp.array([D, D, D, D // 16], jnp.float32)[:, None, None]
    base = jnp.clip(jax.random.normal(key, (4, D, D), jnp.float32), -6.0, 6.0)
    return base * lax.rsqrt(fans)


def draw_vector_weight(key, part):
    key = jax.random.fold_in(key, 7)
    noise_key, bias_key = jax.random.split(key)
    rows = jnp.arange(NVEC)[:, None]
    lanes = jnp.arange(D, dtype=jnp.float32)[None, :] / D
    gain_rows = (rows == 0) | (rows == 2) | (rows == 4) | (rows == 5) | (rows == 7)
    scale_rows = (rows == 13) | (rows == 14)
    tap_rows = (rows >= 15) & (rows < 24)
    rising = 0.6 + 1.2 * lanes
    jitter = jax.random.uniform(noise_key, (NVEC, D), jnp.float32, 0.75, 1.25)
    spread = 0.3 * jnp.clip(jax.random.normal(bias_key, (NVEC, D), jnp.float32), -5.0, 5.0)
    gains = rising * jitter
    scales = jitter - 0.25
    taps = 2.0 * spread
    return jnp.where(gain_rows, gains, jnp.where(scale_rows, scales, jnp.where(tap_rows, taps, spread)))


def levels(rng, dims, cuts, least, largest):
    factor_of = 1.0
    for position, parts in cuts:
        draws = jax.random.uniform(jax.random.fold_in(jax.random.fold_in(rng, 6), position), (parts,), jnp.float32, least / len(cuts), largest / len(cuts))
        factor_of = factor_of * jnp.repeat(jnp.exp(draws), dims[position] // parts).reshape((-1,) + (1,) * (len(dims) - 1 - position))
    return factor_of


def bell_draw(stream_key, extent, scale, reach, cuts=(), kind=jnp.bfloat16):
    loudness = levels(stream_key, extent, cuts, -0.22, 0.18) if cuts else 1.0
    result = jax.random.normal(stream_key, extent, jnp.float32) * scale * loudness
    return jnp.minimum(jnp.maximum(result, -reach), reach).astype(kind)


def setup_inputs(seed: int = 0) -> dict:
    arg_keys = jax.random.split(jax.random.key(seed), 20)
    activations = bell_draw(arg_keys[0], (TOKENS, D), 1.0, 6.0, ((0, 32),))
    cotangent = bell_draw(arg_keys[1], (TOKENS, D), 1.0, 6.0, ((0, 32),), jnp.float32)
    video_length = draw_video_length(jax.random.fold_in(arg_keys[19], 71), 0)
    mix_weight = draw_mix_weight(jax.random.fold_in(arg_keys[19], 71), 0)
    mix_first = bell_draw(arg_keys[4], (4, D, D), (0.0033 / (N_DP * FRAMES_DEV) ** 0.5), 0.00018310547, ((1, 32),), jnp.float32)
    mix_second = jnp.clip(jnp.exp(math.log(5.493163909853216e-11) - 1.3862944 * jax.random.uniform(arg_keys[5], (4, D, D), jnp.float32) ** levels(arg_keys[5], (4, D, D), ((1, 32),), -0.2, 0.2)), 1.373290977463304e-11, 5.493163909853216e-11)
    mix_average = bell_draw(arg_keys[6], (4, D, D), D ** -0.5, 0.25, ((1, 32),), jnp.float32)
    up_weight = bell_draw(arg_keys[7], (D, FF), D ** -0.5, 0.25, ((0, 32),), jnp.float32)
    up_first = bell_draw(arg_keys[8], (D, FF), (0.0033 / (N_DP * FRAMES_DEV) ** 0.5), 0.00018310547, ((0, 32),), jnp.float32)
    up_second = jnp.clip(jnp.exp(math.log(5.493163909853216e-11) - 1.3862944 * jax.random.uniform(arg_keys[9], (D, FF), jnp.float32) ** levels(arg_keys[9], (D, FF), ((0, 32),), -0.2, 0.2)), 1.373290977463304e-11, 5.493163909853216e-11)
    up_average = bell_draw(arg_keys[10], (D, FF), D ** -0.5, 0.25, ((0, 32),), jnp.float32)
    down_weight = bell_draw(arg_keys[11], (FF, D), FF ** -0.5, 0.125, ((0, 32),), jnp.float32)
    down_first = bell_draw(arg_keys[12], (FF, D), (0.0033 / (N_DP * FRAMES_DEV) ** 0.5), 0.00018310547, ((0, 32),), jnp.float32)
    down_second = jnp.clip(jnp.exp(math.log(5.493163909853216e-11) - 1.3862944 * jax.random.uniform(arg_keys[13], (FF, D), jnp.float32) ** levels(arg_keys[13], (FF, D), ((0, 32),), -0.2, 0.2)), 1.373290977463304e-11, 5.493163909853216e-11)
    down_average = bell_draw(arg_keys[14], (FF, D), FF ** -0.5, 0.125, ((0, 32),), jnp.float32)
    vector_weight = draw_vector_weight(jax.random.fold_in(arg_keys[19], 71), 0)
    vector_first = bell_draw(arg_keys[16], (NVEC, D), (0.0132 / (N_DP * FRAMES_DEV) ** 0.5), 0.0007324219, ((1, 32),), jnp.float32)
    vector_second = jnp.clip(jnp.exp(math.log(8.789062255765145e-10) - 1.3862944 * jax.random.uniform(arg_keys[17], (NVEC, D), jnp.float32) ** levels(arg_keys[17], (NVEC, D), ((1, 32),), -0.2, 0.2)), 2.1972655639412864e-10, 8.789062255765145e-10)
    vector_average = bell_draw(arg_keys[18], (NVEC, D), 0.5, 4.0, ((1, 32),), jnp.float32)
    return dict(activations=activations, cotangent=cotangent, video_length=video_length, mix_weight=mix_weight, mix_first=mix_first, mix_second=mix_second, mix_average=mix_average, up_weight=up_weight, up_first=up_first, up_second=up_second, up_average=up_average, down_weight=down_weight, down_first=down_first, down_second=down_second, down_average=down_average, vector_weight=vector_weight, vector_first=vector_first, vector_second=vector_second, vector_average=vector_average)


@jax.custom_vjp
def low(v):
    return lax.optimization_barrier(v.astype(jnp.bfloat16)).astype(jnp.float32)

@jax.custom_vjp
def low_back(v):
    return v

def low_keep(v):
    return (low(v), None)

def low_pass(kept, grad):
    return (grad,)

def back_keep(v):
    return (v, None)

def back_low(kept, grad):
    return (low(grad),)
low.defvjp(low_keep, low_pass)
low_back.defvjp(back_keep, back_low)

def matmul(left, right):
    return jnp.dot(left, right, precision=lax.Precision.HIGHEST)

def layer_norm(value, gain, shift):
    center = value - lax.optimization_barrier(jnp.mean(value, axis=-1, keepdims=True))
    spread = lax.optimization_barrier(jnp.mean(center * center, axis=-1, keepdims=True))
    return center * lax.rsqrt(spread + 1e-05) * gain + shift

def earlier(field, same_prev):
    return jnp.concatenate([jnp.zeros_like(field[:1]), field[:-1]], 0) * same_prev

def later(field, same_next):
    return jnp.concatenate([field[1:], jnp.zeros_like(field[:1])], 0) * same_next

def attention(query, keys_in, values_in, segment):
    block_rows = min(512, FRAMES_DEV)
    radius = WINDOW // 2
    span = block_rows + 2 * radius
    query_heads = query.reshape(FRAMES_DEV, HEADS, HEAD)
    key_pad = jnp.pad(keys_in.reshape(FRAMES_DEV, HEADS, HEAD), ((radius, radius), (0, 0), (0, 0)))
    value_pad = jnp.pad(values_in.reshape(FRAMES_DEV, HEADS, HEAD), ((radius, radius), (0, 0), (0, 0)))
    seg_pad = jnp.pad(segment, (radius, radius), constant_values=-1)
    offset = jnp.arange(span)[None, :] - jnp.arange(block_rows)[:, None]
    in_band = (offset >= 0) & (offset <= 2 * radius)

    def one_block(start):
        query_rows = lax.dynamic_slice_in_dim(query_heads, start, block_rows, 0)
        key_rows = lax.dynamic_slice_in_dim(key_pad, start, span, 0)
        value_rows = lax.dynamic_slice_in_dim(value_pad, start, span, 0)
        seg_rows = lax.dynamic_slice_in_dim(seg_pad, start + radius, block_rows, 0)
        seg_keys = lax.dynamic_slice_in_dim(seg_pad, start, span, 0)
        allowed = (in_band & (seg_rows[:, None] == seg_keys[None, :]))[None]
        scores = low_back(jnp.einsum('qhe,khe->hqk', query_rows, key_rows, precision=lax.Precision.HIGHEST))
        masked = jnp.where(allowed, scores, -1e+30)
        row_top = lax.optimization_barrier(jnp.max(masked, axis=-1, keepdims=True))
        weights = jnp.exp(masked - row_top) * allowed.astype(jnp.float32)
        probs = low(weights / lax.optimization_barrier(jnp.sum(weights, axis=-1, keepdims=True)))
        return jnp.einsum('hqk,khe->qhe', probs, value_rows, precision=lax.Precision.HIGHEST)
    starts = jnp.arange(FRAMES_DEV // block_rows, dtype=jnp.int32) * block_rows
    return lax.map(jax.checkpoint(one_block), starts).reshape(FRAMES_DEV, D)

def forward(frames, mixes, up_matrix, down_matrix, vectors, segment):
    live_mask = (segment < SLOTS).astype(jnp.float32)[:, None]
    same_video = (segment[1:] == segment[:-1]).astype(jnp.float32)
    zero_one = jnp.zeros((1,), jnp.float32)
    same_prev = jnp.concatenate([zero_one, same_video])[:, None]
    same_next = jnp.concatenate([same_video, zero_one])[:, None]
    normed = layer_norm(frames, vectors[0], vectors[1])
    before = earlier(normed, same_prev)
    after_rows = later(normed, same_next)

    def convolve(first_row):
        return live_mask * (vectors[first_row] * before + vectors[first_row + 1] * normed + vectors[first_row + 2] * after_rows)
    query_in = low(layer_norm(convolve(15), vectors[2], vectors[3]))
    key_in = low(layer_norm(convolve(18), vectors[4], 0.0))
    value_in = low(layer_norm(convolve(21), vectors[5], vectors[6]))
    query = low(low_back((matmul(query_in, mixes[0]) + vectors[9]) * HEAD ** (-0.5)))
    keys_out = low(low_back(matmul(key_in, mixes[1])))
    values_out = low(low_back(matmul(value_in, mixes[2]) + vectors[10]))
    attended = low(low_back(attention(query, keys_out, values_out, segment)))
    projected = low_back(matmul(attended, mixes[3]) + vectors[11])
    middle = frames * live_mask + vectors[13] * live_mask * projected
    normed_two = low(layer_norm(middle, vectors[7], vectors[8]))
    hidden_pre = low_back(matmul(normed_two, up_matrix) + vectors[24:].reshape(FF))
    hidden = low(jax.nn.gelu(hidden_pre, approximate=False))
    mlp_out = low_back(matmul(hidden, down_matrix) + vectors[12])
    return middle + vectors[14] * live_mask * mlp_out

def adamw(gradient, weight, moment_one, moment_two, average, rate):
    new_one = 0.9 * moment_one + 0.1 * gradient
    new_two = 0.999 * moment_two + 0.001 * gradient * gradient
    corrected = new_one / (1.0 - 0.9 ** STEP)
    spread = jnp.sqrt(new_two / (1.0 - 0.999 ** STEP)) + 1e-08
    new_weight = weight - rate * (corrected / spread + 0.1 * weight)
    new_average = 0.9 * average + 0.1 * new_weight
    return (new_weight, new_one, new_two, new_average)

def reference(activations, cotangent, video_length, mix_weight, mix_first, mix_second, mix_average, up_weight, up_first, up_second, up_average, down_weight, down_first, down_second, down_average, vector_weight, vector_first, vector_second, vector_average):
    rounded = (low(mix_weight), low(up_weight), low(down_weight), low(vector_weight))
    frames_all = activations.astype(jnp.float32).reshape(GROUPS, FRAMES_DEV, D)
    upstream_all = cotangent.reshape(GROUPS, FRAMES_DEV, D)
    places = jnp.arange(FRAMES_DEV, dtype=jnp.int32)

    def one_group(totals, inputs):
        frames, upstream, lengths = inputs
        video_ends = jnp.cumsum(lengths).astype(jnp.int32)
        segment = lax.optimization_barrier(jnp.sum((places[:, None] >= video_ends[None, :]).astype(jnp.int32), axis=1)).astype(jnp.int32)

        def local(frame_in, mixes, up_matrix, down_matrix, vectors):
            return forward(frame_in, mixes, up_matrix, down_matrix, vectors, segment)
        output, pullback = jax.vjp(local, frames, *rounded)
        pulled = pullback(upstream)
        totals = tuple((summed + piece for summed, piece in zip(totals, pulled[1:])))
        return (totals, (output.astype(jnp.bfloat16), pulled[0]))
    starting = tuple((jnp.zeros_like(weight) for weight in rounded))
    totals, (outputs, input_grads) = lax.scan(one_group, starting, (frames_all, upstream_all, video_length))
    live_total = jnp.sum(video_length).astype(jnp.float32)
    gradients = tuple((summed / live_total for summed in totals))
    square_sum = sum((jnp.sum(gradient * gradient) for gradient in gradients))
    grad_norm = jnp.sqrt(square_sum)
    clip_limit = 0.03 * math.sqrt(NPARAM / (N_DP * FRAMES_DEV))
    clip_factor = clip_limit / jnp.maximum(grad_norm, clip_limit)
    mix_new = adamw(gradients[0] * clip_factor, mix_weight, mix_first, mix_second, mix_average, 0.05)
    up_new = adamw(gradients[1] * clip_factor, up_weight, up_first, up_second, up_average, 0.05)
    down_new = adamw(gradients[2] * clip_factor, down_weight, down_first, down_second, down_average, 0.05)
    vector_new = adamw(gradients[3] * clip_factor, vector_weight, vector_first, vector_second, vector_average, 0.25)
    clipped_bias_grad = gradients[3][12] * clip_factor
    return (outputs.reshape(TOKENS, D), input_grads.reshape(TOKENS, D), grad_norm, mix_new[0], mix_new[1], mix_new[2], mix_new[3], up_new[0], up_new[1], up_new[2], up_new[3], down_new[0], down_new[1], down_new[2], down_new[3], vector_new[0], vector_new[1], vector_new[2], vector_new[3], clipped_bias_grad)
```

```python
import functools
import math

import jax
import jax.numpy as jnp
from jax import lax
from jax.experimental import pallas as pl
from jax.experimental.pallas import tpu as pltpu
from jax.sharding import PartitionSpec as P

HEADS = 4
HEAD = 128
WINDOW = 19
RADIUS = WINDOW // 2
STEP = 10
FRAMES_DEV = 2048
NPARAM = 3160064
D = 512
FF = 2048
ROWS = 256
SUB = 32
PAIR = 128
MID_ROWS = 512
TALL = 64
CHUNK = 256
TILE = 96
HALO = 16
SPAN = TILE + 2 * HALO
FACTOR = HEAD**-0.5
LOG2_E = math.log2(math.e)
F32 = jnp.float32
BF16 = jnp.bfloat16
ANY = pl.BlockSpec(memory_space=pl.ANY)
IN_VMEM = pl.BlockSpec(memory_space=pltpu.VMEM)
IN_SMEM = pl.BlockSpec(memory_space=pltpu.SMEM)
VMEM_LIMIT = 62 * 1024 * 1024


def mm(left, right):
    return jnp.dot(left, right, preferred_element_type=F32)


def mm_nt(left, right):
    return lax.dot_general(left, right, (((1,), (1,)), ((), ())), preferred_element_type=F32)


def normalise(value):
    center = value - jnp.mean(value, axis=-1, keepdims=True)
    scale = lax.rsqrt(jnp.mean(center * center, axis=-1, keepdims=True) + 1e-05)
    return center * scale, scale


def norm_back(upstream, gain, normal, scale):
    inner = upstream * gain
    along = jnp.mean(inner * normal, axis=-1, keepdims=True)
    return scale * (inner - jnp.mean(inner, axis=-1, keepdims=True) - normal * along)


def total(value):
    return jnp.sum(value, axis=0, keepdims=True)


def video_ends(len_ref):
    rank = lax.axis_index("dp")
    first = len_ref[0, rank]
    return first, first + len_ref[1, rank]


def wide(column):
    return jnp.concatenate([column] * (D // 128), axis=1)


def row_index(start):
    return start + lax.broadcasted_iota(jnp.int32, (SUB, 128), 0)


def live_rows(start, ends):
    return wide((row_index(start) < ends[1]).astype(F32))


def copy_all(pairs, sems):
    copies = [pltpu.make_async_copy(src, dst, sems.at[i]) for i, (src, dst) in enumerate(pairs)]
    for copy in copies:
        copy.start()
    return copies


def attention_mask(start, ends, frames):
    t = start + lax.broadcasted_iota(jnp.int32, (TILE, SPAN), 0)
    u = start - HALO + lax.broadcasted_iota(jnp.int32, (1, SPAN), 1)
    one, none = jnp.int32(64), jnp.int32(0)

    def code(spot):
        return (
            spot
            + jnp.where(spot >= ends[0], one, none)
            + jnp.where(spot >= ends[1], one, none)
            + jnp.where(spot >= frames, one, none)
        )

    return jnp.abs(code(t) - (code(u) + jnp.where(u < 0, -one, none))) <= RADIUS


def inside(spot, ends, frames):
    first = (spot == 0) | (spot == ends[0]) | (spot == ends[1])
    last = (spot == frames - 1) | (spot == ends[0] - 1) | (spot == ends[1] - 1)
    return wide(1.0 - first.astype(F32)), wide(1.0 - last.astype(F32))


def shifted(window, size, spot, ends, frames):
    not_first, not_last = inside(spot, ends, frames)
    return window[7 : size + 7] * not_first, window[8 : size + 8], window[9 : size + 9] * not_last


def slot_of(owner):
    z, y, x, core = owner // 8, owner // 4 % 2, owner // 2 % 2, owner % 2
    return ((core * 2 + y) * 2 + x) * 4 + z


def whole_matrix(slots, rows, cols=slice(None)):
    return jnp.concatenate([slots[slot_of(owner), rows, cols] for owner in range(D // WIDTH)], axis=0)


def early_matrix(early, j):
    return whole_matrix(early, slice(j * WIDTH, (j + 1) * WIDTH))


def front_kernel(near, len_ref, x_in, *refs):
    if near:
        mix_ref, up_ref, down_ref, wvec_ref, vec_ref, up_out, down_out, *refs = refs
    else:
        early, vec_ref, *refs = refs
    outs, refs = refs[:8], refs[8:]
    kept, refs = refs[:8], refs[8:]
    xh, x3, rs, n3t, qkv, wt, p, o = kept
    x, low, sems, *refs = refs
    q, kp, vp = (qkv.at[j] for j in range(3))
    frames = x.shape[0]
    tiles = p.shape[0] // TILE
    steps = frames // ROWS
    ends = video_ends(len_ref)
    load = pltpu.make_async_copy(x_in, x, sems.at[8])
    load.start()
    if near:
        early, up_slots, down_slots, tables, *refs = refs
        z, y, x_, core = place()
        me = ((core * 2 + y) * 2 + x_) * 4 + z
        greet()
        tables[me, :, 0 : wvec_ref.shape[1]] = wvec_ref[...].astype(BF16)
        first = Gather(tables, refs[0])
        first.start_z()
        for j in range(3):
            early[me, j * WIDTH : (j + 1) * WIDTH, :] = mix_ref[j].astype(BF16)
        second = Gather(early, refs[1])
        second.start_z()
        up_slots[me, 0:WIDTH, :] = mix_ref[3].astype(BF16)
        for c in range(FF // D):
            up_slots[me, (c + 1) * WIDTH : (c + 2) * WIDTH, :] = up_ref[:, c * D : (c + 1) * D].astype(BF16)
        third = Gather(up_slots, refs[2])
        third.start_z()
        down_slots[me] = down_ref[...].astype(BF16)
        fourth = Gather(down_slots, refs[3])
        fourth.start_z()
    zero8 = jnp.zeros((8, D), F32)
    xh[0:8, :] = zero8
    xh[frames + 8 : frames + 16, :] = zero8
    q[frames:, :] = jnp.zeros((q.shape[0] - frames, D), BF16)
    for ref in (kp, vp):
        ref[0:HALO, :] = jnp.zeros((HALO, D), BF16)
        ref[frames + HALO :, :] = jnp.zeros((ref.shape[0] - frames - HALO, D), BF16)
    load.wait()

    def norm_step(i, carry):
        for s in range(PAIR // SUB):
            start = pl.multiple_of(i * PAIR + s * SUB, SUB)
            normal, scale = normalise(x[pl.ds(start, SUB), :].astype(F32))
            xh[pl.ds(start + 8, SUB), :] = normal
            rs[pl.ds(start, SUB), :] = jnp.broadcast_to(scale, (SUB, 128))
        return carry

    lax.fori_loop(0, frames // PAIR, norm_step, 0)
    copies = [pltpu.make_async_copy(kept[i], outs[i], sems.at[i]) for i in range(6)]
    copies[0].start()
    if near:
        first.all_along_z()
        first.all_arrive()
        second.along_z()
        table = whole_matrix(tables, slice(None))
    else:
        table = whole_matrix(early, slice(3 * WIDTH, None), slice(0, 128))
    table = table.astype(F32).T
    vec_ref[...] = table[0 : vec_ref.shape[0]]

    marks = (frames // PAIR * 3 // 8, frames // PAIR * 3 // 4)

    def conv_step(i, carry):
        if near:

            @pl.when(i == marks[0])
            def _():
                second.in_plane()

            @pl.when(i == marks[1])
            def _():
                second.diagonal()

        for s in range(PAIR // SUB):
            start = pl.multiple_of(i * PAIR + s * SUB, SUB)
            rows = pl.ds(start, SUB)
            live = live_rows(start, ends)
            window = xh[pl.ds(start, SUB + 16), :] * vec_ref[0:1, :] + vec_ref[1:2, :]
            before, own, after = shifted(window, SUB, row_index(start), ends, frames)
            scales = []
            for j, (gain, shift, taps) in enumerate(((2, 3, 15), (4, None, 18), (5, 6, 21))):
                conv = live * (
                    vec_ref[taps : taps + 1, :] * before
                    + vec_ref[taps + 1 : taps + 2, :] * own
                    + vec_ref[taps + 2 : taps + 3, :] * after
                )
                normal, scale = normalise(conv)
                scales.append(scale)
                x3[j, rows, :] = normal
                normed = normal * vec_ref[gain : gain + 1, :]
                if shift is not None:
                    normed = normed + vec_ref[shift : shift + 1, :]
                low[j, rows, :] = normed.astype(BF16)
            lane = lax.broadcasted_iota(jnp.int32, (SUB, 128), 1)
            scale = rs[rows, :]
            for j in range(3):
                scale = jnp.where(lane == j, scales[j], scale)
            rs[rows, :] = scale
        return carry

    def project_step(i, carry):
        top = pl.multiple_of(i * ROWS, ROWS)
        rows = pl.ds(top, ROWS)
        padded = pl.ds(top + HALO, ROWS)
        nq, nk, nv = (low[j, rows, :] for j in range(3))
        q[rows, :] = ((mm(nq, early_matrix(early, 0)) + vec_ref[9:10, :]) * FACTOR).astype(BF16)
        kp[padded, :] = mm(nk, early_matrix(early, 1)).astype(BF16)
        vp[padded, :] = (mm(nv, early_matrix(early, 2)) + vec_ref[10:11, :]).astype(BF16)
        n3t[0, :, rows] = nq.T
        n3t[1, :, rows] = nk.T
        n3t[2, :, rows] = nv.T
        return carry

    lax.fori_loop(0, frames // PAIR, conv_step, 0)
    for i in (1, 2):
        copies[i].start()
    if near:
        third.along_z()
        second.arrive()
    lax.fori_loop(0, steps, project_step, 0)
    if near:
        fourth.along_z()
    for j in range(3):
        wt[j] = early_matrix(early, j).T
    for i in (3, 4, 5):
        copies[i].start()

    def attend(start):
        allowed = attention_mask(start, ends, frames)
        heads = [slice(head * HEAD, (head + 1) * HEAD) for head in range(HEADS)]
        scores = [mm_nt(q[pl.ds(start, TILE), cols], kp[pl.ds(start, SPAN), cols]) for cols in heads]
        masked = [jnp.where(allowed, score, -1e30) for score in scores]
        tops = [jnp.max(score, axis=-1, keepdims=True) for score in masked]
        weights = [jnp.exp2((score - top) * LOG2_E) for score, top in zip(masked, tops)]
        sums = [jnp.sum(weight, axis=-1, keepdims=True) for weight in weights]
        probs = [weight * pltpu.reciprocal(count, approx=True) for weight, count in zip(weights, sums)]
        for prob, cols in zip(probs, heads):
            p[pl.ds(start, TILE), cols] = prob
        mixed = [mm(prob.astype(BF16), vp[pl.ds(start, SPAN), cols]) for prob, cols in zip(probs, heads)]
        for value, cols in zip(mixed, heads):
            o[pl.ds(start, TILE), cols] = value.astype(BF16)

    pairs = tiles // 2
    most = pairs * 3 // 4
    leaving = [
        pltpu.make_async_copy(kept[j].at[rows], outs[j].at[rows], sems.at[9 + 2 * k + j - 6])
        for k, rows in enumerate((pl.ds(0, most * 2 * TILE), pl.ds(most * 2 * TILE, (pairs - most) * 2 * TILE)))
        for j in (6, 7)
    ]

    def attend_step(i, carry):
        if near:

            @pl.when(i == pairs // 4)
            def _():
                third.in_plane()

            @pl.when(i == pairs // 2)
            def _():
                third.diagonal()
                fourth.in_plane()

            @pl.when(i == pairs - 2)
            def _():
                fourth.diagonal()

        @pl.when(i == most)
        def _():
            for copy in leaving[:2]:
                copy.start()

        for k in range(2):
            attend(pl.multiple_of((2 * i + k) * TILE, 32))
        return carry

    lax.fori_loop(0, pairs, attend_step, 0)
    parts = leaving
    for copy in leaving[2:]:
        copy.start()
    if near:
        third.arrive()
        up_copy = pltpu.make_async_copy(up_slots, up_out, sems.at[13])
        up_copy.start()
        fourth.arrive()
        down_copy = pltpu.make_async_copy(down_slots, down_out, sems.at[14])
        down_copy.start()
        for part in (first, second, third, fourth):
            part.sent_all()
        parts = parts + [up_copy, down_copy]
    for copy in copies + parts:
        copy.wait()


def front(near, lengths, x, weights):
    frames = x.shape[0]
    tiles = -(-frames // TILE)
    padded = tiles * TILE
    spread = (tiles - 1) * TILE + SPAN
    owners = D // WIDTH
    dma = pltpu.SemaphoreType.DMA
    shapes = [
        ((frames + 16, D), F32),
        ((3, frames, D), F32),
        ((frames, 128), F32),
        ((3, D, frames), BF16),
        ((3, spread, D), BF16),
        ((3, D, D), BF16),
        ((padded, D), F32),
        ((padded, D), BF16),
    ]
    outs = [((32, D), F32)]
    scratch = shapes + [((frames, D), BF16), ((3, frames, D), BF16)]
    scratch = [pltpu.VMEM(shape, kind) for shape, kind in scratch] + [dma((15,))]
    params = dict(vmem_limit_bytes=VMEM_LIMIT)
    if near:
        outs += [((owners, UP, D), BF16), ((owners, DOWN, D), BF16)]
        scratch += [pltpu.VMEM((owners, *slot), BF16) for slot in ((3 * WIDTH, D), (UP, D), (DOWN, D), (WIDTH, 128))]
        scratch += [dma((6,))] * 4
        params.update(collective_id=0, has_side_effects=True)
    return pl.pallas_call(
        functools.partial(front_kernel, near),
        out_shape=[jax.ShapeDtypeStruct(shape, kind) for shape, kind in outs + shapes],
        in_specs=[IN_SMEM, ANY] + [IN_VMEM] * len(weights),
        out_specs=[IN_VMEM] + [ANY] * (len(outs) - 1 + len(shapes)),
        scratch_shapes=scratch,
        compiler_params=pltpu.CompilerParams(**params),
        name="front",
    )(lengths, x, *weights)


def gelu_pair(z):
    phi = lax.erf(z * math.sqrt(0.5)) * 0.5 + 0.5
    bell = jnp.exp2(z * z * (-0.5 * LOG2_E))
    return z * phi, phi + z * bell * (1.0 / math.sqrt(2.0 * math.pi))


def fold(value):
    return jnp.sum(value.reshape(value.shape[0] // 8, 8, value.shape[1]), axis=0)


def deal(sums, rows, value, first=0):
    size = rows.stop - rows.start
    for k in range(value.shape[0] // size):
        slot = slot_of(first + k)
        sums[slot // 16, slot % 16, rows, :] = value[k * size : (k + 1) * size].astype(sums.dtype)


def middle_kernel(
    len_ref, o_in, x_in, dy_in, vec_ref, up_in, down_in,
    out_out, dx_out, do_out, up_out, down_out, gvec,
    o, x, dy, out, up_sums, down_sums, slots, down_slots, gel, dz1, n2t, dz2t, ot, da, keep_pj, keep_mid, keep_xh, keep_r,
    acc, in_sems, row_sems, out_sems,
):
    frames = x.shape[0]
    steps = frames // MID_ROWS
    ends = video_ends(len_ref)
    load_slots = [
        pltpu.make_async_copy(src, dst, in_sems.at[i]) for i, (src, dst) in enumerate(((up_in, slots), (down_in, down_slots)))
    ]
    cut = MID_ROWS
    row_loads = [
        [
            pltpu.make_async_copy(src.at[rows], dst.at[rows], row_sems.at[k, half])
            for k, (src, dst) in enumerate(((o_in, o), (x_in, x), (dy_in, dy)))
        ]
        for half, rows in enumerate((pl.ds(0, cut), pl.ds(cut, frames - cut)))
    ]
    for load in [row_loads[0][0], *load_slots, *row_loads[0][1:], *row_loads[1]]:
        load.start()
    acc[...] = jnp.zeros_like(acc)
    for load in load_slots + row_loads[0]:
        load.wait()

    def add(row, value):
        acc[row] += fold(value)

    def up_rows(c):
        return slice((c + 1) * WIDTH, (c + 2) * WIDTH)

    def down_rows(start, size):
        each = 4 * WIDTH
        return jnp.concatenate([down_slots[slot_of(k)] for k in range(start // each, (start + size) // each)], axis=0)

    def step(i, carry):
        top = pl.multiple_of(i * MID_ROWS, MID_ROWS)
        all_rows = pl.ds(top, MID_ROWS)

        @pl.when(i == 1)
        def _():
            for load in row_loads[1]:
                load.wait()

        s1, s2 = vec_ref[13:14, :], vec_ref[14:15, :]
        ot[:, all_rows] = o[all_rows, :].T
        n2, dz2 = [None, None], [None, None]

        def half_rows(h):
            return pl.ds(pl.multiple_of(top + h * ROWS, ROWS), ROWS)

        def project(h):
            return mm(o[half_rows(h), :], whole_matrix(slots, slice(0, WIDTH)))

        def norm_half(h, projected):
            low_n2, low_dz2 = [], []
            for s in range(ROWS // SUB):
                start = pl.multiple_of(top + h * ROWS + s * SUB, SUB)
                rows, here = pl.ds(start, SUB), slice(h * ROWS + s * SUB, h * ROWS + (s + 1) * SUB)
                live = live_rows(start, ends)
                value = projected[s * SUB : (s + 1) * SUB] + vec_ref[11:12, :]
                keep_pj[here, :] = value
                mid = live * (x[rows, :].astype(F32) + s1 * value)
                keep_mid[here, :] = mid
                normal, scale = normalise(mid)
                keep_xh[here, :] = normal
                keep_r[here, :] = jnp.broadcast_to(scale, (SUB, 128))
                low_n2.append((normal * vec_ref[7:8, :] + vec_ref[8:9, :]).astype(BF16))
                low = (s2 * (live * dy[rows, :])).astype(BF16)
                add(4, low.astype(F32))
                low_dz2.append(low)
            n2[h], dz2[h] = jnp.concatenate(low_n2, axis=0), jnp.concatenate(low_dz2, axis=0)

        def back_blocks(h, z2, dn2, blocks):
            for s in blocks:
                start = pl.multiple_of(top + h * ROWS + s * SUB, SUB)
                rows, here = pl.ds(start, SUB), slice(h * ROWS + s * SUB, h * ROWS + (s + 1) * SUB)
                spot = slice(s * SUB, (s + 1) * SUB)
                live = live_rows(start, ends)
                z2_live = live * (z2[spot] + vec_ref[12:13, :])
                out[rows, :] = (keep_mid[here, :] + s2 * z2_live).astype(BF16)
                dy_rows = dy[rows, :]
                add(5, dy_rows * z2_live)
                normal = keep_xh[here, :]
                up = dn2[spot]
                add(0, up * normal)
                add(1, up)
                dx1 = dy_rows + norm_back(up, vec_ref[7:8, :], normal, keep_r[here, 0:1])
                dy[rows, :] = dx1
                dx_live = dx1 * live
                add(2, dx_live * keep_pj[here, :])
                low = (s1 * dx_live).astype(BF16)
                add(3, low.astype(F32))
                da[rows, :] = low

        def back_dot(h):
            o[half_rows(h), :] = mm_nt(da[half_rows(h), :], whole_matrix(slots, slice(0, WIDTH))).astype(BF16)

        def z2_dot(h):
            return mm(gel[half_rows(h), :], down_rows(0, FF))

        def dn2_dot(h):
            return sum(
                mm_nt(dz1[half_rows(h), c * D : (c + 1) * D], whole_matrix(slots, up_rows(c))) for c in range(FF // D)
            )

        projected = [project(0), project(1)]
        norm_half(0, projected[0])

        units = [(c, h) for c in range(FF // CHUNK) for h in range(MID_ROWS // ROWS)]

        def inner(c):
            return slice(c * CHUNK % D, c * CHUNK % D + CHUNK)

        def up_dot(c, h):
            return mm(n2[h], whole_matrix(slots, up_rows(c * CHUNK // D), inner(c)))

        def down_dot(c, h):
            return mm_nt(dz2[h], down_rows(c * CHUNK, CHUNK))

        def activate(c, h, z1, dgel, blocks):
            cols = slice(c * CHUNK, (c + 1) * CHUNK)
            big = c * CHUNK // D
            for s in blocks:
                here = slice(s * TALL, (s + 1) * TALL)
                rows = pl.ds(pl.multiple_of(top + h * ROWS + s * TALL, TALL), TALL)
                value, slope = gelu_pair(z1[here] + vec_ref[24 + big : 25 + big, inner(c)])
                gel[rows, cols] = value.astype(BF16)
                back = dgel[here] * slope
                dz1[rows, cols] = back.astype(BF16)
                acc[8 + big, :, inner(c)] += fold(back)

        count = ROWS // TALL
        blocks = ROWS // SUB
        z1, dgel = up_dot(*units[0]), down_dot(*units[0])
        norm_half(1, projected[1])
        for h in range(2):
            n2t[:, half_rows(h)] = n2[h].T
            dz2t[:, half_rows(h)] = dz2[h].T
        z2 = dn2 = None
        for u, unit in enumerate(units):
            following = units[u + 1] if u + 1 < len(units) else None
            if following:
                next_z1 = up_dot(*following)
            else:
                z2 = z2_dot(0)
            activate(*unit, z1, dgel, range(count // 2))
            if following:
                next_dgel = down_dot(*following)
            else:
                dn2 = dn2_dot(0)
            activate(*unit, z1, dgel, range(count // 2, count))
            z1, dgel = next_z1, next_dgel
        next_z2 = z2_dot(1)
        back_blocks(0, z2, dn2, range(blocks // 2))
        next_dn2 = dn2_dot(1)
        back_blocks(0, z2, dn2, range(blocks // 2, blocks))
        back_dot(0)
        back_blocks(1, next_z2, next_dn2, range(blocks))
        back_dot(1)
        return carry

    lax.fori_loop(0, steps, step, 0)
    o[frames:, :] = jnp.zeros((o.shape[0] - frames, D), BF16)
    gvec[...] = jnp.sum(acc[...], axis=1)
    pairs = [(out, out_out), (dy, dx_out), (o, do_out), (up_sums, up_out), (down_sums, down_out)]
    copies = [pltpu.make_async_copy(src, dst, out_sems.at[i]) for i, (src, dst) in enumerate(pairs)]
    for copy in copies[:3]:
        copy.start()
    deal(up_sums, slice(0, WIDTH), mm(ot[...], da[...]))
    for c in range(FF // D):
        deal(up_sums, slice((c + 1) * WIDTH, (c + 2) * WIDTH), mm(n2t[...], dz1[:, c * D : (c + 1) * D]))
    copies[3].start()
    for c in range(FF // D):
        turned = mm(dz2t[...], gel[:, c * D : (c + 1) * D])
        turned = turned.astype(BF16).T if down_sums.dtype == BF16 else turned.T
        deal(down_sums, slice(0, DOWN), turned, 8 * c)
    copies[4].start()
    for copy in copies:
        copy.wait()


def middle(near, lengths, o, x, dy, vectors, up, down):
    frames = x.shape[0]
    padded = o.shape[0]
    owners = up.shape[0]
    outs = [
        ((frames, D), BF16),
        ((frames, D), F32),
        ((padded, D), BF16),
        ((2, owners // 2, UP, D), BF16 if near else F32),
        ((2, owners // 2, DOWN, D), BF16 if near else F32),
        ((16, D), F32),
    ]
    scratch = [
        ((padded, D), BF16),
        ((frames, D), BF16),
        ((frames, D), F32),
        ((frames, D), BF16),
        ((2, owners // 2, UP, D), BF16 if near else F32),
        ((2, owners // 2, DOWN, D), BF16 if near else F32),
        ((owners, UP, D), BF16),
        ((owners, DOWN, D), BF16),
        ((frames, FF), BF16),
        ((frames, FF), BF16),
        ((D, frames), BF16),
        ((D, frames), BF16),
        ((D, frames), BF16),
        ((frames, D), BF16),
        ((MID_ROWS, D), F32),
        ((MID_ROWS, D), F32),
        ((MID_ROWS, D), F32),
        ((MID_ROWS, 128), F32),
        ((16, 8, D), F32),
    ]
    return pl.pallas_call(
        middle_kernel,
        out_shape=[jax.ShapeDtypeStruct(shape, kind) for shape, kind in outs],
        in_specs=[IN_SMEM, ANY, ANY, ANY, IN_VMEM, ANY, ANY],
        out_specs=[ANY] * 5 + [IN_VMEM],
        scratch_shapes=[pltpu.VMEM(shape, kind) for shape, kind in scratch]
        + [pltpu.SemaphoreType.DMA(shape) for shape in ((2,), (3, 2), (5,))],
        compiler_params=pltpu.CompilerParams(vmem_limit_bytes=VMEM_LIMIT),
        name="middle",
    )(lengths, o, x, dy, vectors, up, down)


def back_kernel(near, len_ref, vec_ref, gmid_ref, *refs):
    if near:
        up_in, down_in, *refs = refs
    saved, refs = refs[:7], refs[7:]
    do_in, dx_in, ig_out, *refs = refs
    if near:
        early_part, up_part, down_part, vec_part, square, *refs = refs
    else:
        early_sums, gvec, *refs = refs
    rs, n3t, qkv, wt, p, xh, triple, do, refs = *refs[:8], refs[8:]
    carry_k, carry_v, acc, unit, ups, in_sems, part_sems, out_sems, *refs = refs
    q, kp, vp = (qkv.at[j] for j in range(3))
    frames = xh.shape[0] - 16
    tiles = p.shape[0] // TILE
    ends = video_ends(len_ref)
    body = pl.ds(8, frames)
    dx = p.at[0:frames]
    xh_in, x3_in, rs_in, n3t_in, qkv_in, wt_in, p_in = saved
    pairs = [(n3t_in, n3t), (wt_in, wt), (xh_in, xh), (rs_in, rs), (x3_in, triple.at[:, body]), (dx_in, dx)]
    copies = [pltpu.make_async_copy(src, dst, in_sems.at[i]) for i, (src, dst) in enumerate(pairs)]
    pairs = tiles // 2
    cut = 2 * 2 * TILE
    segments = []
    for half, (top, end) in enumerate(((0, cut), (cut, 2 * pairs * TILE))):
        rows = pl.ds(top, end - top)
        spread = pl.ds(top + 2 * HALO * half, end - top + 2 * HALO * (1 - half))
        arrays = [(qkv_in.at[0], q, rows), (qkv_in.at[1], kp, spread), (qkv_in.at[2], vp, spread)]
        arrays += [(do_in, do, rows), (p_in, p, rows)]
        segments.append(
            [
                pltpu.make_async_copy(src.at[part], dst.at[part], part_sems.at[half, j])
                for j, (src, dst, part) in enumerate(arrays)
            ]
        )
    for copy in segments[0]:
        copy.start()
    if near:
        up_refs, down_refs, early_refs, tail_refs = refs[:12], refs[12:24], refs[24:36], refs[36:]
        core = lax.axis_index("dp") % 2
        loads = [
            pltpu.make_async_copy(src.at[half], refs[0].at[half], in_sems.at[6 + k])
            for k, (src, refs, half) in enumerate(
                (
                    (up_in, up_refs, 1 - core), (down_in, down_refs, 1 - core),
                    (up_in, up_refs, core), (down_in, down_refs, core),
                )
            )
        ]
        loads[0].start()
        loads[1].start()
        greet()
        up_sum, down_sum, early_sum = RelayScatter(*up_refs), RelayScatter(*down_refs), RelayScatter(*early_refs)
        tail = Tail(*tail_refs)
        loads[0].wait()
        up_sum.to_core()
        loads[1].wait()
        down_sum.to_core()
        loads[2].start()
        loads[3].start()
        early_sums = early_refs[0]
    for copy in segments[1]:
        copy.start()
    carry_k[...] = jnp.zeros_like(carry_k)
    carry_v[...] = jnp.zeros_like(carry_v)
    acc[...] = jnp.zeros_like(acc)
    ij = [lax.broadcasted_iota(jnp.int32, unit.shape, k) for k in range(2)]
    unit[...] = (ij[0] == ij[1]).astype(F32).astype(BF16)
    zero8 = jnp.zeros((8, D), F32)
    for j in range(3):
        triple[j, 0:8, :] = zero8
        triple[j, frames + 8 : frames + 16, :] = zero8

    def attend(tile, span):
        heads = [slice(head * HEAD, (head + 1) * HEAD) for head in range(HEADS)]
        probs = [p[tile, cols] for cols in heads]
        d_probs = [mm_nt(do[tile, cols], vp[span, cols]) for cols in heads]
        inner = [jnp.sum(pr * dp, axis=-1, keepdims=True) for pr, dp in zip(probs, d_probs)]
        d_scores = [(pr * (dp - mean)).astype(BF16) for pr, dp, mean in zip(probs, d_probs, inner)]
        turned = [mm_nt(unit[...], pr.astype(BF16)).astype(BF16) for pr in probs]
        dvs = [mm(pr, do[tile, cols]) for pr, cols in zip(turned, heads)]
        dqs = [mm(ds, kp[span, cols]) for ds, cols in zip(d_scores, heads)]
        turned = [mm_nt(unit[...], ds).astype(BF16) for ds in d_scores]
        dks = [mm(ds, q[tile, cols]) for ds, cols in zip(turned, heads)]
        return dqs, dks, dvs

    def attend_step(i, carry):
        @pl.when(i == 2)
        def _():
            for copy in segments[1]:
                copy.wait()

        @pl.when(i == pairs // 4)
        def _():
            if near:
                loads[2].wait()
                up_sum.to_plane()
            for copy in copies[0:4]:
                copy.start()

        @pl.when(i == pairs // 2)
        def _():
            if near:
                loads[3].wait()
                down_sum.to_plane()

        @pl.when(i == pairs - 2)
        def _():
            if near:
                up_sum.relay()
            copies[4].start()

        starts = [pl.multiple_of((2 * i + k) * TILE, 32) for k in range(2)]
        results = [attend(pl.ds(start, TILE), pl.ds(start, SPAN)) for start in starts]
        start = starts[0]
        for head in range(HEADS):
            cols = slice(head * HEAD, (head + 1) * HEAD)
            for which, held, ref in ((1, carry_k, kp), (2, carry_v, vp)):
                one, two = (result[which][head] for result in results)
                ref[pl.ds(start, 32), cols] = (one[0:32] + held[:, cols]).astype(BF16)
                ref[pl.ds(start + 32, TILE - 32), cols] = one[32:TILE].astype(BF16)
                ref[pl.ds(start + TILE, 32), cols] = (one[TILE:SPAN] + two[0:32]).astype(BF16)
                ref[pl.ds(start + TILE + 32, TILE - 32), cols] = two[32:TILE].astype(BF16)
                held[:, cols] = two[TILE:SPAN]
            for k in range(2):
                q[pl.ds(starts[k], TILE), cols] = results[k][0][head].astype(BF16)
        return carry

    for copy in segments[0]:
        copy.wait()
    lax.fori_loop(0, pairs, attend_step, 0)
    if near:
        down_sum.relay()
    copies[5].start()
    copies[0].wait()
    spans = [slice(j * WIDTH, (j + 1) * WIDTH) for j in range(3)]
    deal(early_sums, spans[0], mm(n3t[0], q[0:frames, :]) * FACTOR)
    deal(early_sums, spans[1], mm(n3t[1], kp[HALO : HALO + frames, :]))
    if near:
        up_sum.to_z()
    deal(early_sums, spans[2], mm(n3t[2], vp[HALO : HALO + frames, :]))
    if near:
        early_sum.to_core()
        down_sum.to_z()
    for copy in copies[1:5]:
        copy.wait()

    def add(row, value):
        acc[row] += fold(value)

    def norm_tile(i, carry):
        if near:

            @pl.when(i == steps // 4)
            def _():
                early_sum.to_plane()

            @pl.when(i == steps * 5 // 8)
            def _():
                early_sum.relay()

            @pl.when(i == steps - 1)
            def _():
                early_sum.to_z()

        top = pl.multiple_of(i * ROWS, ROWS)
        padded = pl.ds(top + HALO, ROWS)
        for j, low in enumerate((q[pl.ds(top, ROWS), :], kp[padded, :], vp[padded, :])):
            ups[j] = mm(low, wt[j])

        def step(k, carry):
            return norm_step(top, k, carry)

        return lax.fori_loop(0, ROWS // PAIR, step, carry)

    def norm_step(top, k, carry):
        for s in range(PAIR // SUB):
            offset = pl.multiple_of(k * PAIR + s * SUB, SUB)
            start = pl.multiple_of(top + offset, SUB)
            here, rows, body = pl.ds(offset, SUB), pl.ds(start, SUB), pl.ds(start + 8, SUB)
            lows = {0: q[rows, :], 2: vp[pl.ds(start + HALO, SUB), :]}
            live = (row_index(start) < ends[1]).astype(F32)[:, 0:1]
            not_first, not_last = inside(row_index(start), ends, frames)
            window = xh[pl.ds(start, SUB + 16), :]
            before, own, after = window[7 : SUB + 7], window[8 : SUB + 8], window[9 : SUB + 9]
            spread = [0.0, 0.0, 0.0]
            for j, (gain, taps) in enumerate(((2, 15), (4, 18), (5, 21))):
                upstream = ups[j, here, :]
                gains = vec_ref[gain : gain + 1, :]
                if j == 0:
                    gains = gains * FACTOR
                    add(9, lows[j].astype(F32))
                elif j == 2:
                    add(10, lows[j].astype(F32))
                normal = triple[j, body, :]
                add(gain, upstream * normal)
                if j != 1:
                    add(gain + 1, upstream)
                masked = norm_back(upstream, gains, normal, rs[rows, j : j + 1] * live)
                masked_first, masked_last = masked * not_first, masked * not_last
                add(taps, masked_first * before)
                add(taps + 1, masked * own)
                add(taps + 2, masked_last * after)
                add(taps + 9, masked_first)
                add(taps + 10, masked)
                add(taps + 11, masked_last)
                spread[0] = spread[0] + vec_ref[taps : taps + 1, :] * masked_first
                spread[1] = spread[1] + vec_ref[taps + 1 : taps + 2, :] * masked
                spread[2] = spread[2] + vec_ref[taps + 2 : taps + 3, :] * masked_last
            for tap in range(3):
                triple[tap, body, :] = spread[tap]
        return carry

    steps = frames // ROWS
    lax.fori_loop(0, steps, norm_tile, 0)

    sums = jnp.sum(acc[...], axis=1)
    along, plain, taps = sums[15:24], sums[24:33], vec_ref[15:24, :]
    table = jnp.concatenate(
        [
            total(taps * along),
            total(taps * plain),
            sums[2:4] * FACTOR,
            sums[4:7],
            gmid_ref[0:2, :],
            sums[9:10] * FACTOR,
            sums[10:11],
            gmid_ref[3:5, :],
            gmid_ref[2:3, :],
            gmid_ref[5:6, :],
            vec_ref[0:1, :] * along + vec_ref[1:2, :] * plain,
            gmid_ref[8:12, :],
        ],
        axis=0,
    )
    if near:
        turned = jnp.concatenate([table, jnp.zeros((128 - table.shape[0], D), F32)], axis=0).T
        tail.start(turned)
    else:
        gvec[...] = table
    copies[5].wait()

    early_rows = frames * 3 // 4
    leave = [
        pltpu.make_async_copy(dx.at[rows], ig_out.at[rows], out_sems.at[i])
        for i, rows in enumerate((pl.ds(0, early_rows), pl.ds(early_rows, frames - early_rows)))
    ]

    def input_step(i, carry):
        if near:

            @pl.when(i == frames // PAIR // 4)
            def _():
                up_sum.finish()

            @pl.when(i == frames // PAIR * 3 // 4)
            def _():
                down_sum.finish()

        @pl.when(i == early_rows // PAIR)
        def _():
            leave[0].start()

        for s in range(PAIR // SUB):
            start = pl.multiple_of(i * PAIR + s * SUB, SUB)
            rows = pl.ds(start, SUB)
            live = live_rows(start, ends)
            later = triple[0, pl.ds(start + 8, SUB + 8), :][1 : SUB + 1]
            earlier = triple[2, pl.ds(start, SUB + 8), :][7 : SUB + 7]
            d_normed = triple[1, pl.ds(start + 8, SUB), :] + later + earlier
            normal = xh[pl.ds(start + 8, SUB), :]
            dx[rows, :] = live * dx[rows, :] + norm_back(d_normed, vec_ref[0:1, :], normal, rs[rows, 3:4])
        return carry

    lax.fori_loop(0, frames // PAIR, input_step, 0)
    leave[1].start()
    if near:
        up_part[...] = up_sum.result[...]
        down_part[...] = down_sum.result[...]
        early_sum.finish()
        early_part[...] = early_sum.result[...]
        lanes = 0.0
        for ref in (early_part, up_part, down_part):
            squares = total(ref[...] * ref[...])
            lanes = lanes + sum(squares[:, c * 128 : (c + 1) * 128] for c in range(D // 128))
        tail.along_z(lanes)
        vec_part[...], lanes = tail.finish()
        square[...] = jnp.broadcast_to(jnp.sum(lanes, axis=1, keepdims=True), (8, 128))
        for part in (up_sum, down_sum, early_sum, tail):
            part.sent_all()
    for copy in leave:
        copy.wait()


def back(near, lengths, vectors, sums_middle, later_sums, saved, do, dx):
    frames = dx.shape[0]
    half = D // WIDTH // 2
    dma = pltpu.SemaphoreType.DMA
    rows = 3 * WIDTH
    outs = [((frames, D), F32)]
    if near:
        outs += [((rows, D), F32), ((UP, D), F32), ((DOWN, D), F32), ((WIDTH, 128), F32), ((8, 128), F32)]
    else:
        outs += [((2, half, rows, D), F32), ((28, D), F32)]
    scratch = [(array.shape, array.dtype) for array in saved[2:]]
    scratch += [
        ((frames + 16, D), F32),
        ((3, frames + 16, D), F32),
        (do.shape, BF16),
        ((32, D), F32),
        ((32, D), F32),
        ((33, 8, D), F32),
        ((SPAN, HEAD), BF16),
        ((3, ROWS, D), F32),
    ]
    scratch = [pltpu.VMEM(shape, kind) for shape, kind in scratch] + [dma((10,)), dma((2, 5)), dma((2,))]
    params = dict(vmem_limit_bytes=VMEM_LIMIT)
    if near:
        scratch += RelayScatter.scratch(UP, D) + RelayScatter.scratch(DOWN, D) + RelayScatter.scratch(rows, D)
        scratch += Tail.scratch()
        params.update(collective_id=1, has_side_effects=True)
    else:
        later_sums = ()
    return pl.pallas_call(
        functools.partial(back_kernel, near),
        out_shape=[jax.ShapeDtypeStruct(shape, kind) for shape, kind in outs],
        in_specs=[IN_SMEM, IN_VMEM, IN_VMEM] + [ANY] * (len(later_sums) + len(saved) + 2),
        out_specs=[ANY] + [IN_VMEM] * (len(outs) - 1),
        scratch_shapes=scratch,
        compiler_params=pltpu.CompilerParams(**params),
        name="back",
    )(lengths, vectors, sums_middle, *later_sums, *saved, do, dx)


MESH = pl.DeviceIdType.MESH
PLANE = ((0, 1), (1, 0), (1, 1))
WIDTH = 16
UP = 5 * WIDTH
DOWN = 4 * WIDTH


def place():
    me = lax.axis_index("dp")
    return me // 8, (me // 4) % 2, (me // 2) % 2, me % 2


def index_of(z, y, x, core):
    return ((z * 2 + y) * 2 + x) * 2 + core


def plane_partner(step):
    z, y, x, core = place()
    return index_of(z, (y + step[0]) % 2, (x + step[1]) % 2, core)


def core_partner():
    z, y, x, core = place()
    return index_of(z, y, x, 1 - core)


def z_partner(step):
    z, y, x, core = place()
    return index_of((z + step) % 4, y, x, core)


def remote(src, dst, send_sem, recv_sem, device):
    return pltpu.make_async_remote_copy(
        src_ref=src, dst_ref=dst, send_sem=send_sem, recv_sem=recv_sem, device_id=(device,), device_id_type=MESH
    )


def flat_place():
    z, y, x, core = place()
    return (core * 2 + y) * 2 + x


def flat_partner(k):
    spot = (flat_place() + k) % 8
    return spot, index_of(place()[0], spot // 2 % 2, spot % 2, spot // 4)


def near_partners():
    return [z_partner(step) for step in (1, 2, 3)] + [flat_partner(k)[1] for k in range(1, 8)]


def greet():
    barrier = pltpu.get_barrier_semaphore()
    partners = near_partners()
    for partner in partners:
        pl.semaphore_signal(barrier, inc=1, device_id=(partner,), device_id_type=MESH)
    pl.semaphore_wait(barrier, len(partners))


def arrived(part, sem):
    remote(part, part, sem, sem, core_partner()).wait_recv()


def left(part, sem):
    remote(part, part, sem, sem, core_partner()).wait_send()


class Tail:
    def __init__(self, columns, inbox, z_out, z_box, norm_box, sems):
        self.columns, self.inbox, self.z_out, self.z_box, self.norm_box = columns, inbox, z_out, z_box, norm_box
        self.sems = sems

    @staticmethod
    def scratch():
        shapes = [(8, WIDTH, 128), (8, WIDTH, 128), (WIDTH + 8, 128), (4, WIDTH + 8, 128), (8, 8, 128)]
        return [pltpu.VMEM(shape, F32) for shape in shapes] + [pltpu.SemaphoreType.DMA((6,))]

    def send(self, k, src, dst, device):
        remote(src, dst, self.sems.at[3 + k], self.sems.at[k], device).start()

    def start(self, turned):
        for spot in range(8):
            tile = 0.0
            for z in range(4):
                owner = ((z * 2 + spot // 2 % 2) * 2 + spot % 2) * 2 + spot // 4
                part = turned[owner * WIDTH : (owner + 1) * WIDTH]
                tile = tile + (pltpu.roll(part, 32 * z, 1) if z else part)
            self.columns[spot] = tile
        own = flat_place()
        self.inbox[own] = self.columns[own]
        for k in range(1, 8):
            spot, device = flat_partner(k)
            self.send(0, self.columns.at[spot], self.inbox.at[own], device)

    def along_z(self, squares):
        z = place()[0]
        arrived(self.inbox.at[pl.ds(0, 7)], self.sems.at[0])
        self.z_out[0:WIDTH, :] = jnp.sum(self.inbox[...], axis=0)
        self.z_out[WIDTH:, :] = jnp.broadcast_to(squares, (8, 128))
        self.z_box[z] = self.z_out[...]
        for k in range(3):
            self.send(1, self.z_out, self.z_box.at[z], z_partner(k + 1))

    def finish(self):
        z, own = place()[0], flat_place()
        arrived(self.z_box.at[pl.ds(0, 3)], self.sems.at[1])
        whole = jnp.sum(self.z_box[...], axis=0)
        column = whole[0:WIDTH]
        squares = total(column * column) + whole[WIDTH : WIDTH + 1]
        self.norm_box[own] = jnp.broadcast_to(squares, (8, 128))
        for k in range(1, 8):
            self.send(2, self.norm_box.at[own], self.norm_box.at[own], flat_partner(k)[1])
        part = jnp.where(z == 0, column, 0.0)
        for k in range(1, 4):
            part = part + jnp.where(z == k, pltpu.roll(column, 128 - 32 * k, 1), 0.0)
        arrived(self.norm_box.at[pl.ds(0, 7)], self.sems.at[2])
        return part, jnp.sum(self.norm_box[...], axis=0)

    def sent_all(self):
        for k, part in enumerate((self.inbox.at[pl.ds(0, 7)], self.z_box.at[pl.ds(0, 3)], self.norm_box.at[pl.ds(0, 7)])):
            left(part, self.sems.at[3 + k])


class Gather:
    def __init__(self, slots, sems):
        self.slots, self.sems = slots, sems

    def slot(self):
        z, y, x, core = place()
        return self.slots.at[((core * 2 + y) * 2 + x) * 4 + z]

    def column(self, step=(0, 0), start=0, size=4):
        z, y, x, core = place()
        base = ((core * 2 + (y + step[0]) % 2) * 2 + (x + step[1]) % 2) * 4
        return self.slots.at[pl.ds(base + start, size)]

    def send(self, k, part, device):
        remote(part, part, self.sems.at[5], self.sems.at[k], device).start()

    def wait(self, k, size):
        arrived(self.slots.at[pl.ds(0, size)], self.sems.at[k])

    def start_z(self):
        for k in range(3):
            self.send(0, self.slot(), z_partner(k + 1))

    def along_z(self):
        self.wait(0, 3)
        own = self.column()
        for k in range(2):
            self.send(1 + k, own, plane_partner(PLANE[k]))
        self.send(4, own, core_partner())

    def in_plane(self):
        for k in range(2):
            self.wait(1 + k, 4)
            self.send(3, self.column(PLANE[k], start=2 * k, size=2), plane_partner(PLANE[1 - k]))
            self.send(4, self.column(PLANE[k]), core_partner())

    def diagonal(self):
        self.wait(3, 4)
        self.send(4, self.column(PLANE[2]), core_partner())

    def all_along_z(self):
        self.wait(0, 3)
        for k in range(1, 8):
            self.send(1, self.column(), flat_partner(k)[1])

    def all_arrive(self):
        self.wait(1, 28)

    def arrive(self):
        self.wait(4, 16)

    def sent_all(self):
        left(self.slots.at[pl.ds(0, 31)], self.sems.at[5])


class RelayScatter:
    def __init__(self, sums, core_in, ahead_out, ahead_in, after_out, after_in, z_out, z_in, held, whole, *rest):
        self.sums, self.core_in = sums, core_in
        self.ahead_out, self.ahead_in, self.after_out, self.after_in = ahead_out, ahead_in, after_out, after_in
        self.z_out, self.z_in, self.held, self.whole = z_out, z_in, held, whole
        self.result, self.sems = rest

    @staticmethod
    def scratch(rows, lanes):
        counts = [(2, 16), (16,), (2, 4), (2, 4), (2, 2), (2, 2), (3,), (3,), (4,)]
        return (
            [pltpu.VMEM((*count, rows, lanes), BF16) for count in counts]
            + [pltpu.VMEM((4, rows, lanes), F32), pltpu.VMEM((rows, lanes), F32)]
            + [pltpu.SemaphoreType.DMA((8,))]
        )

    def send(self, k, src, dst, device):
        remote(src, dst, self.sems.at[4 + k], self.sems.at[k], device).start()

    def blocks(self, work):
        def step(r, carry):
            work(pl.ds(pl.multiple_of(r * WIDTH, WIDTH), WIDTH))
            return carry

        lax.fori_loop(0, self.result.shape[0] // WIDTH, step, 0)

    def to_core(self):
        self.send(0, self.sums.at[1 - place()[3]], self.core_in, core_partner())

    def to_plane(self):
        arrived(self.core_in, self.sems.at[0])
        z, y, x, core = place()

        def both(step, zz, rows):
            chip = ((y + step[0]) % 2 * 2 + (x + step[1]) % 2) * 4 + zz
            return self.sums[core, chip, rows, :] + self.core_in[chip, rows, :]

        for k in range(2):

            def pack(rows):
                for half in range(2):
                    self.ahead_out[k, half, rows, :] = both(PLANE[2], 2 * k + half, rows)
                    self.ahead_out[k, 2 + half, rows, :] = both(PLANE[k], 2 * k + half, rows)

            self.blocks(pack)
            self.send(1, self.ahead_out.at[k], self.ahead_in.at[k], plane_partner(PLANE[k]))

        def keep(rows):
            for k in range(2):
                for half in range(2):
                    self.after_out[k, half, rows, :] = both(PLANE[k], 2 * (1 - k) + half, rows)
                    self.held[2 * k + half, rows, :] = both((0, 0), 2 * k + half, rows)

        self.blocks(keep)

    def relay(self):
        arrived(self.ahead_in, self.sems.at[1])
        for k in range(2):

            def pack(rows):
                for half in range(2):
                    at = (k, half, rows, slice(None))
                    self.after_out[at] = self.after_out[at] + self.ahead_in[1 - k, half, rows, :]

            self.blocks(pack)
            self.send(2, self.after_out.at[k], self.after_in.at[k], plane_partner(PLANE[k]))

    def to_z(self):
        z, y, x, core = place()
        arrived(self.after_in, self.sems.at[2])

        def add(rows):
            for k in range(2):
                for half in range(2):
                    value = self.held[2 * k + half, rows, :].astype(F32) + self.ahead_in[k, 2 + half, rows, :].astype(F32)
                    self.whole[2 * k + half, rows, :] = value + self.after_in[1 - k, half, rows, :].astype(F32)

        self.blocks(add)

        def pack(rows):
            for k in range(3):
                self.z_out[k, rows, :] = self.whole[(z + k + 1) % 4, rows, :].astype(BF16)
            self.result[rows, :] = self.whole[z, rows, :]

        self.blocks(pack)
        for k in range(3):
            self.send(3, self.z_out.at[k], self.z_in.at[k], z_partner(k + 1))

    def finish(self):
        arrived(self.z_in, self.sems.at[3])

        def add(rows):
            value = self.result[rows, :]
            for k in range(3):
                value = value + self.z_in[k, rows, :].astype(F32)
            self.result[rows, :] = value

        self.blocks(add)

    def sent_all(self):
        for k, part in enumerate((self.core_in, self.ahead_in, self.after_in, self.z_in)):
            left(part, self.sems.at[4 + k])


def update_kernel(len_ref, ig_in, early_part, up_part, down_part, vec_part, square, *refs):
    state_in, norm_out, bias_out, refs = refs[:16], refs[16], refs[17], refs[18:]
    state_out, ig_out, state, new, refs = refs[:16], refs[16], refs[17:33], refs[33:49], refs[49:]
    passing, state_sems, new_sems, in_sems, out_sems = refs
    pieces = in_sems.shape[0]
    size = ig_in.shape[0] // pieces
    parts = [slice(i * size, (i + 1) * size) for i in range(pieces)]
    loads = copy_all(zip(state_in, state), state_sems)
    ig_loads = copy_all([(ig_in.at[part], passing.at[part]) for part in parts], in_sems)
    ig_stores = [
        pltpu.make_async_copy(passing.at[part], ig_out.at[part], out_sems.at[i]) for i, part in enumerate(parts)
    ]
    stores = [pltpu.make_async_copy(new[i], state_out[i], new_sems.at[i]) for i in range(16)]
    n = len_ref.shape[1]
    live = lax.fori_loop(0, n, lambda i, count: count + len_ref[0, i] + len_ref[1, i], jnp.int32(0))
    share = 1.0 / jnp.full((8, 128), live, jnp.int32).astype(F32)
    norm = jnp.sqrt(square[...]) * share
    limit = 0.03 * math.sqrt(NPARAM / (n * FRAMES_DEV))
    factor = (limit / jnp.maximum(norm, limit) * share)[0:1, 0:1]
    norm_out[...] = norm[0:1, 0:1]
    turned = jnp.concatenate([vec_part[...], jnp.zeros((128 - WIDTH, 128), F32)], axis=0).T
    bias_out[...] = turned[12:13, 0:WIDTH] * factor

    def apply(gradient, which, at, rate):
        weight, one, two, average = (state[4 * which + j][at] for j in range(4))
        result = adamw(gradient * factor, weight, one, two, average, rate)
        for j in range(4):
            new[4 * which + j][at] = result[j]

    for which in range(4):
        for load in loads[4 * which : 4 * which + 4]:
            load.wait()
        if which == 0:
            for j in range(3):
                apply(early_part[j * WIDTH : (j + 1) * WIDTH, :], 0, j, 0.05)
            apply(up_part[0:WIDTH, :], 0, 3, 0.05)
        elif which == 1:
            for c in range(FF // D):
                at = (slice(None), slice(c * D, (c + 1) * D))
                apply(up_part[(1 + c) * WIDTH : (2 + c) * WIDTH, :], 1, at, 0.05)
        elif which == 2:
            apply(down_part[...], 2, slice(None), 0.05)
        else:
            apply(vec_part[:, 0 : state[12].shape[1]], 3, slice(None), 0.25)
        for store in stores[4 * which : 4 * which + 4]:
            store.start()
        for i in range(which * pieces // 4, (which + 1) * pieces // 4):
            ig_loads[i].wait()
            ig_stores[i].start()
    for store in stores + ig_stores:
        store.wait()


def update(lengths, input_grad, parts, state):
    small = [jax.ShapeDtypeStruct(shape, F32) for shape in ((1, 1), (1, WIDTH))]
    large = [jax.ShapeDtypeStruct(array.shape, F32) for array in (*state, input_grad)]
    dma = pltpu.SemaphoreType.DMA
    results = pl.pallas_call(
        update_kernel,
        out_shape=small + large,
        in_specs=[IN_SMEM, ANY] + [IN_VMEM] * len(parts) + [ANY] * len(state),
        out_specs=[IN_VMEM] * 2 + [ANY] * len(large),
        scratch_shapes=[pltpu.VMEM(array.shape, F32) for array in (*state, *state, input_grad)]
        + [dma((16,)), dma((16,)), dma((4,)), dma((4,))],
        compiler_params=pltpu.CompilerParams(vmem_limit_bytes=VMEM_LIMIT),
        name="update",
    )(lengths, input_grad, *parts, *state)
    return (*results[2:18], results[0], results[1], results[18])


def adamw(gradient, weight, moment_one, moment_two, average, rate):
    new_one = 0.9 * moment_one + 0.1 * gradient
    new_two = 0.999 * moment_two + 0.001 * gradient * gradient
    corrected = new_one / (1.0 - 0.9**STEP)
    spread = jnp.sqrt(new_two / (1.0 - 0.999**STEP)) + 1e-08
    new_weight = weight - rate * (corrected / spread + 0.1 * weight)
    new_average = 0.9 * average + 0.1 * new_weight
    return (new_weight, new_one, new_two, new_average)


def to_slots(array):
    array = array.reshape(4, 2, 2, 2, *array.shape[1:])
    return array.transpose(3, 1, 2, 0, *range(4, array.ndim)).reshape(-1, *array.shape[4:])


def to_owners(array):
    array = array.reshape(2, 2, 2, 4, *array.shape[2:])
    return array.transpose(3, 1, 2, 0, *range(4, array.ndim)).reshape(-1, *array.shape[4:])


def pack_weights(mixes, up, down, vectors):
    owners = D // WIDTH
    table = jnp.pad(vectors.T, ((0, 0), (0, D - vectors.shape[0])))
    early = [matrix.reshape(owners, WIDTH, D) for matrix in (mixes[0], mixes[1], mixes[2], table)]
    later = [matrix.reshape(owners, WIDTH, D) for matrix in (mixes[3], *jnp.split(up, FF // D, axis=1))]
    slots = (jnp.concatenate(early, axis=1), jnp.concatenate(later, axis=1), down.reshape(owners, DOWN, D))
    return tuple(to_slots(array) for array in slots)


def body(
    activations,
    cotangent,
    video_length,
    mix_weight,
    mix_first,
    mix_second,
    mix_average,
    up_weight,
    up_first,
    up_second,
    up_average,
    down_weight,
    down_first,
    down_second,
    down_average,
    vector_weight,
    vector_first,
    vector_second,
    vector_average,
):
    groups = lax.axis_size("dp")
    near = groups == 32
    lengths = video_length.T
    if near:
        weights = (mix_weight, up_weight, down_weight, vector_weight.T)
        vectors, up, down, *saved = front(near, lengths, activations, weights)
    else:
        early, up, down = pack_weights(
            lax.all_gather(mix_weight.astype(BF16), "dp", axis=1, tiled=True),
            lax.all_gather(up_weight.astype(BF16), "dp", axis=0, tiled=True),
            lax.all_gather(down_weight.astype(BF16), "dp", axis=0, tiled=True),
            lax.all_gather(vector_weight.astype(BF16), "dp", axis=1, tiled=True),
        )
        vectors, *saved = front(near, lengths, activations, (early,))
    attended = saved.pop()
    block_output, d_middle, d_attended, *later_sums, sums_middle = middle(
        near, lengths, attended, activations, cotangent, vectors, up, down
    )
    input_grad, *sums = back(near, lengths, vectors, sums_middle, later_sums, saved, d_attended, d_middle)
    if near:
        state = (
            mix_weight, mix_first, mix_second, mix_average, up_weight, up_first, up_second, up_average,
            down_weight, down_first, down_second, down_average,
            vector_weight.T, vector_first.T, vector_second.T, vector_average.T,
        )
        *new_state, grad_norm, clipped, input_grad = update(lengths, input_grad, sums, state)
        new_state[12:] = [array.T for array in new_state[12:]]
        return (block_output, input_grad, grad_norm.reshape(()), *new_state, clipped.reshape(-1))
    early_sum = to_owners(sums[0]).reshape(-1, 3, WIDTH, D)
    up_sum, down_sum = (to_owners(array) for array in later_sums)
    vector_grad = sums[1]
    mix_grad = jnp.stack(
        [early_sum[:, j].reshape(D, D) for j in range(3)] + [up_sum[:, 0:WIDTH].reshape(D, D)]
    )
    grad_up = jnp.concatenate(
        [up_sum[:, (c + 1) * WIDTH : (c + 2) * WIDTH].reshape(D, D) for c in range(FF // D)], axis=1
    )
    grad_down = down_sum.reshape(FF, D)
    live_total = jnp.sum(video_length).astype(F32)
    mix_part = lax.psum_scatter(mix_grad, "dp", scatter_dimension=1, tiled=True) / live_total
    up_part = lax.psum_scatter(grad_up, "dp", scatter_dimension=0, tiled=True) / live_total
    down_part = lax.psum_scatter(grad_down, "dp", scatter_dimension=0, tiled=True) / live_total
    vector_part = lax.psum_scatter(vector_grad, "dp", scatter_dimension=1, tiled=True) / live_total
    square_sum = lax.psum(
        jnp.sum(mix_part * mix_part)
        + jnp.sum(up_part * up_part)
        + jnp.sum(down_part * down_part)
        + jnp.sum(vector_part * vector_part),
        "dp",
    )
    grad_norm = jnp.sqrt(square_sum)
    clip_limit = 0.03 * math.sqrt(NPARAM / (groups * FRAMES_DEV))
    clip_factor = clip_limit / jnp.maximum(grad_norm, clip_limit)
    mix_new = adamw(mix_part * clip_factor, mix_weight, mix_first, mix_second, mix_average, 0.05)
    up_new = adamw(up_part * clip_factor, up_weight, up_first, up_second, up_average, 0.05)
    down_new = adamw(
        down_part * clip_factor, down_weight, down_first, down_second, down_average, 0.05
    )
    vector_new = adamw(
        vector_part * clip_factor, vector_weight, vector_first, vector_second, vector_average, 0.25
    )
    clipped_bias_grad = vector_part[12] * clip_factor
    return (
        block_output,
        input_grad,
        grad_norm,
        *mix_new,
        *up_new,
        *down_new,
        *vector_new,
        clipped_bias_grad,
    )


def solution(mesh):
    state = [P(None, "dp", None)] * 4 + [P("dp", None)] * 8 + [P(None, "dp")] * 4
    rows = P("dp", None)
    return jax.shard_map(
        body,
        mesh=mesh,
        in_specs=(rows, rows, P(), *state),
        out_specs=(rows, rows, P(), *state, P("dp")),
        check_vma=False,
    )
```
